256 devices in a mesh: expert: 32 (over z, y), dp: 8 (over x, core).
Axes of the slice: x: 4, y: 4, z: 8, core: 2. Of those that a mesh axis runs over, the one named last changes fastest.
Arguments:
- tokens: bfloat16 [4096, 7168], P(('expert', 'dp')), may hold values from -6 to 6
- grad_out: bfloat16 [4096, 7168], P(('expert', 'dp')), may hold values from -4 to 4
- routes: int32 [4096, 8], P(('expert', 'dp')), may hold values from 0 to 31, all different within a row; in each aligned block of 16 rows (0 to 15, 16 to 31, ...) at most 5 rows name the same one
- gates: bfloat16 [4096, 8], P(('expert', 'dp')), may hold values from 0.049804688 to 0.5
- w_up: bfloat16 [32, 7168, 1024], P('expert', 'dp'), may hold values from -0.0625 to 0.0625
- w_down: bfloat16 [32, 1024, 7168], P('expert', None, 'dp'), may hold values from -0.1875 to 0.1875
Outputs:
- grad_tokens: bfloat16 [4096, 7168], P(('expert', 'dp'))
- grad_gates: float32 [4096, 8], P(('expert', 'dp'))
- grad_up: bfloat16 [32, 7168, 1024], P('expert', 'dp')
- grad_down: bfloat16 [32, 1024, 7168], P('expert', None, 'dp')
The draws below stay inside these ranges and needn't reach their ends.
Inputs may be any that keep to these rules, and one draw needn't show every extreme that they name: `routes`: each row names 8 different experts. Within the 16 rows of one device no expert is named by more than 5 rows, and in every draw some expert is named exactly 5 times by the rows of some device.
All inputs are finite; a program needn't handle non-finite values.
Results may differ from the reference program's by a relative error of at most 0.023.
Values may be sent and summed in bfloat16 or wider, within the bound.
A program may use at most 128 MiB of HBM per device.

```python
import math
import jax
import jax.numpy as jnp
import numpy as np
from jax import lax

D = 7168
FF = 1024
TOPK = 8
TOK_DEV = 16
EXPERTS = 32
CAP = 5
TOKENS = 4096
N_EXPERT = 32
N_DP = 8


def level_of(rng, shape, shards, low, high):
    def one(axis_at, blocks):
        draws = jax.random.uniform(jax.random.fold_in(jax.random.fold_in(rng, 6), axis_at), (blocks,), jnp.float32, low / len(shards), high / len(shards))
        return jnp.repeat(jnp.exp(draws), shape[axis_at] // blocks).reshape((-1,) + (1,) * (len(shape) - axis_at - 1))

    level = one(*shards[0])
    for cut in shards[1:]:
        level = level * one(*cut)
    return level


def deal_out(rng, own, number, rows, count, top, most, skew):
    ranking = jax.random.permutation(rng, count)
    crowded, ordinary = portions_of(count, rows * top, most, skew, True), portions_of(count, rows * top, most, skew, False)
    places = jnp.arange(count)

    def named(tallies, offset_by):
        used = int((tallies > 0).sum())
        fixed = max(1, used // 4)
        moved = fixed + (places - fixed + offset_by * (used - fixed)) % max(1, count - fixed)
        return jnp.zeros((count,), jnp.int32).at[ranking[jnp.where(places < fixed, places, moved)]].set(jnp.asarray(tallies, jnp.int32))

    tallies = jnp.where(number % 4 == 0, named(crowded, number // 4), named(ordinary, number - number // 4 - 1))
    mixed = jax.random.permutation(jax.random.fold_in(own, 3), count)
    source_of, taker = mixed[0:count // 2 * 2:2], mixed[1:count // 2 * 2:2]
    room = jnp.minimum(tallies[source_of] - 1, most - tallies[taker]) // 2
    room = jnp.where((source_of == ranking[0]) | (taker == ranking[0]) | (tallies[taker] == 0), 0, jnp.maximum(room, 0))
    moved = jax.random.randint(jax.random.fold_in(own, 4), (count // 2,), 0, 1 << 20) % (room + 1)
    tallies = tallies.at[source_of].add(-moved).at[taker].add(moved)
    labels = jnp.searchsorted(jnp.cumsum(tallies), jnp.arange(rows * top), side="right").astype(jnp.int32)
    grid = labels.reshape(top, rows).T
    grid = grid[jax.random.permutation(jax.random.fold_in(own, 1), rows)]
    offset_by = jax.random.randint(jax.random.fold_in(own, 2), (rows, 1), 0, top)
    return jnp.take_along_axis(grid, (jnp.arange(top)[None, :] + offset_by) % top, axis=1)


def portions_of(amount, total, reach, skew, full):
    loads = [(1 << 20) // math.isqrt(grade ** skew) + 1 for grade in range(1, amount + 1)]
    largest = reach if full else min(reach, max(-(-total // amount), total * loads[0] // sum(loads)))
    least = 1 if total - largest >= amount - 1 else 0
    given, spare = [largest] + [least] * (amount - 1), total - largest - least * (amount - 1)
    while spare > 0:
        candidates = [i for i in range(1, amount) if given[i] < largest] or [i for i in range(1, amount) if given[i] < reach]
        whole, remaining = sum([loads[i] for i in candidates]), spare
        for i in candidates:
            addition = min(reach - given[i], max(1, remaining * loads[i] // whole), spare)
            given[i] = given[i] + addition
            spare = spare - addition
    return np.array(given)


def bell_draw(own_key, dims, spread, reach, split=(), kind=jnp.bfloat16):
    entries = spread * jax.random.normal(own_key, dims, jnp.float32)
    if split:
        entries = entries * level_of(own_key, dims, split, -0.22, 0.18)
    return jnp.clip(entries, -reach, reach).astype(kind)


def setup_inputs(seed: int = 0) -> dict:
    key_of = jax.random.split(jax.random.key(seed), 7)
    tokens = bell_draw(key_of[0], (TOKENS, D), 1.0, 6.0, ((0, 256),))
    grad_out = bell_draw(key_of[1], (TOKENS, D), 0.5, 4.0, ((0, 256),))
    routes_keys = jax.random.split(jax.random.fold_in(key_of[2], 1), TOKENS // TOK_DEV)
    routes_turns = jax.random.permutation(jax.random.fold_in(key_of[2], 3), TOKENS // TOK_DEV)
    routes = jax.vmap(lambda own, number: deal_out(jax.random.fold_in(key_of[2], 2), own, number, TOK_DEV, EXPERTS, TOPK, CAP, 2))(routes_keys, routes_turns).reshape((TOKENS, TOPK))
    gates = jnp.clip(jnp.exp(math.log(0.5) - 2.306499 * jax.random.uniform(key_of[3], (TOKENS, TOPK), jnp.float32) ** level_of(key_of[3], (TOKENS, TOPK), ((0, 256),), -0.2, 0.2)), 0.049804688, 0.5).astype(jnp.bfloat16)
    w_up = bell_draw(key_of[4], (EXPERTS, D, FF), D ** -0.5, 0.0625, ((0, 32), (1, 8)))
    w_down = bell_draw(key_of[5], (EXPERTS, FF, D), FF ** -0.5, 0.1875, ((0, 32), (2, 8)))
    return {"tokens": tokens, "grad_out": grad_out, "routes": routes, "gates": gates, "w_up": w_up, "w_down": w_down}


def silu_slope(values):
    sigma = jax.nn.sigmoid(values)
    return sigma * (1.0 + values * (1.0 - sigma))


def rounded_sum(parts):
    rounded = lax.optimization_barrier(parts.astype(jnp.bfloat16))
    return jnp.sum(rounded.astype(jnp.float32), axis=0)


def reference(tokens, grad_out, routes, gates, w_up, w_down):
    route_total = TOKENS * TOPK
    dev_total = N_EXPERT * N_DP
    feat_width = D // N_DP
    slot_total = dev_total * CAP
    flat_routes = routes.reshape(route_total).astype(jnp.int32)
    route_ids = jnp.arange(route_total, dtype=jnp.int32)
    device_ids = (route_ids // (TOK_DEV * TOPK)).astype(jnp.int32)
    onehot = (flat_routes.reshape(dev_total, TOK_DEV * TOPK)[:, :, None] == jnp.arange(EXPERTS, dtype=jnp.int32)[None, None, :]).astype(jnp.int32)
    rank_table = jnp.cumsum(onehot, axis=1) - onehot
    rank_of = jnp.sum(rank_table * onehot, axis=2).reshape(route_total).astype(jnp.int32)
    slot_route = jnp.full((EXPERTS, dev_total, CAP), -1, jnp.int32).at[flat_routes, device_ids, rank_of].set(route_ids)
    slot_route = slot_route.reshape(EXPERTS, slot_total)
    gate_flat = gates.reshape(route_total)

    def per_expert(state_pair, inputs):
        token_grad, gate_grad = state_pair
        slot_list, up_weight, down_weight = inputs
        is_live = slot_list >= 0
        safe_index = jnp.where(is_live, slot_list, 0).astype(jnp.int32)
        token_index = (safe_index // TOPK).astype(jnp.int32)
        live_rows = is_live[:, None]
        in_rows = jnp.where(live_rows, tokens[token_index], jnp.zeros((), jnp.bfloat16))
        grad_rows = jnp.where(live_rows, grad_out[token_index], jnp.zeros((), jnp.bfloat16))
        gate_rows = jnp.where(is_live, gate_flat[safe_index], jnp.zeros((), jnp.bfloat16))
        up_parts = jnp.einsum("rbi,bif->brf", in_rows.astype(jnp.float32).reshape(slot_total, N_DP, feat_width), up_weight.astype(jnp.float32).reshape(N_DP, feat_width, FF), precision=lax.Precision.HIGHEST)
        pre = rounded_sum(up_parts)
        hidden = jax.nn.silu(pre).astype(jnp.bfloat16)
        expert_out = jnp.dot(hidden, down_weight, preferred_element_type=jnp.float32)
        gate_dots = jnp.sum(expert_out * grad_rows.astype(jnp.float32), axis=1)
        scaled = (gate_rows.astype(jnp.float32)[:, None] * grad_rows.astype(jnp.float32)).astype(jnp.bfloat16)
        back_parts = jnp.einsum("rbi,fbi->brf", scaled.astype(jnp.float32).reshape(slot_total, N_DP, feat_width), down_weight.astype(jnp.float32).reshape(FF, N_DP, feat_width), precision=lax.Precision.HIGHEST)
        back = rounded_sum(back_parts)
        slope = (back * silu_slope(pre)).astype(jnp.bfloat16)
        route_grad = jnp.dot(slope, up_weight.T, preferred_element_type=jnp.float32)
        up_grad = jnp.dot(in_rows.T, slope, preferred_element_type=jnp.float32).astype(jnp.bfloat16)
        down_grad = jnp.dot(hidden.T, scaled, preferred_element_type=jnp.float32).astype(jnp.bfloat16)
        token_grad = token_grad.at[token_index].add(jnp.where(live_rows, route_grad, jnp.float32(0.0)))
        gate_grad = gate_grad.at[safe_index].add(jnp.where(is_live, gate_dots, jnp.float32(0.0)))
        return (token_grad, gate_grad), (up_grad, down_grad)

    start_pair = (jnp.zeros((TOKENS, D), jnp.float32), jnp.zeros((route_total,), jnp.float32))
    (token_grad, gate_grad), (grad_up, grad_down) = lax.scan(per_expert, start_pair, (slot_route, w_up, w_down))
    return token_grad.astype(jnp.bfloat16), gate_grad.reshape(TOKENS, TOPK), grad_up, grad_down
```

```python
import functools

import jax
import jax.numpy as jnp
from jax import lax
from jax.experimental import pallas as pl
from jax.experimental.pallas import tpu as pltpu
from jax.sharding import PartitionSpec as P

MESH = pl.DeviceIdType.MESH
BF = jnp.bfloat16
F32 = jnp.float32

NZ, NY, NX, NC = 8, 4, 4, 2
CAP = 5
PAIRS = ((0, 1), (7, 2), (6, 3), (5, 4))
POS = {k: 2 * s + i for s, pair in enumerate(PAIRS) for i, k in enumerate(pair)}
HALF = 512


def dot(a, b, ca, cb):
    return lax.dot_general(a, b, (((ca,), (cb,)), ((), ())), preferred_element_type=F32)


class Sems:
    def __init__(self, send, recv):
        self.send, self.recv, self.used, self.started = send, recv, 0, []

    def copy(self, src, dst, device):
        i = self.used
        self.used += 1
        cp = pltpu.make_async_remote_copy(
            src, dst, self.send.at[i], self.recv.at[i], device_id=device, device_id_type=MESH
        )
        cp.start()
        self.started.append(cp)
        return cp


def kernel(
    tok, go, meta, wu_h, wd_h,
    gt, gg, gu_h, gd_h,
    ag_t, ag_g, low, sel, gsel, st_t, st_g, rows_t, rows_g, wu, wd,
    own, cs, cr, rs_s, rs_r, pre_sh, gdot, hid, slp,
    st_r, ret, part, zs, zr, fin, fr, gst,
    sems_s, sems_r, sems_l,
):
    e, d = lax.axis_index("expert"), lax.axis_index("dp")
    z, y, x, c = e // NY, e % NY, d // NC, d % NC
    n_dp = NX * NC
    T, D = tok.shape
    F, FF = wu.shape
    G = T * n_dp
    SG = CAP * n_dp
    CH = 2 * SG
    RP = NY * CH
    TM = ag_t.shape[2]

    def zdev(o):
        return (((z + o + NZ) % NZ) * NY + y, d)

    def ydev(o):
        return (z * NY + (y + o + NY) % NY, d)

    def xdev(o):
        return (e, ((x + o) % NX) * NC + c)

    core = (e, x * NC + (1 - c))

    def dpdev(o):
        return (e, (d + o) % n_dp)

    bar = pltpu.get_barrier_semaphore()
    peers = [dpdev(o) for o in range(1, n_dp)] + [zdev(1), zdev(-1)] + [ydev(o) for o in range(1, NY)]
    for p in peers:
        pl.semaphore_signal(bar, inc=1, device_id=p, device_id_type=MESH)
    load_u = pltpu.make_async_copy(wu_h, wu, sems_l.at[0])
    load_d = pltpu.make_async_copy(wd_h, wd, sems_l.at[1])
    load_u.start()
    load_d.start()
    pl.semaphore_wait(bar, len(peers))
    S = Sems(sems_s, sems_r)

    my_rows = pl.ds(pl.multiple_of(d * T, T), T)
    in_t, in_g = [], []
    for o in range(1, n_dp):
        cols = pl.ds(pl.multiple_of(((d + o) % n_dp) * F, 128), F)
        in_t.append(S.copy(meta, ag_t.at[0, my_rows, pl.ds(F, 128)], dpdev(o)))
        in_t.append(S.copy(tok.at[:, cols], ag_t.at[0, my_rows, pl.ds(0, F)], dpdev(o)))
    for o in range(1, n_dp):
        cols = pl.ds(pl.multiple_of(((d + o) % n_dp) * F, 128), F)
        in_g.append(S.copy(go.at[:, cols], ag_g.at[0, my_rows], dpdev(o)))
    mine = pl.ds(pl.multiple_of(d * F, 128), F)
    loc = [
        pltpu.make_async_copy(meta, ag_t.at[0, my_rows, pl.ds(F, 128)], sems_l.at[2]),
        pltpu.make_async_copy(tok.at[:, mine], ag_t.at[0, my_rows, pl.ds(0, F)], sems_l.at[3]),
        pltpu.make_async_copy(go.at[:, mine], ag_g.at[0, my_rows], sems_l.at[4]),
    ]
    for cp in loc:
        cp.start()
    ri = lax.broadcasted_iota(jnp.int32, (2 * G, 2 * G), 0)
    ci = lax.broadcasted_iota(jnp.int32, (2 * G, 2 * G), 1)
    same = (ri >> 4) == (ci >> 4)
    low[...] = jnp.where(same & (ci < ri), 1.0, 0.0).astype(BF)

    def forward(ag, h):
        up, down = h, (NZ - h) % NZ
        width = ag.shape[2]
        if h == 3:
            a, b = pl.ds(0, HALF), pl.ds(HALF, width - HALF)
            return [
                S.copy(ag.at[POS[up], :, a], ag.at[POS[4], :, a], zdev(1)),
                S.copy(ag.at[POS[down], :, b], ag.at[POS[4], :, b], zdev(-1)),
            ]
        return [
            S.copy(ag.at[POS[up]], ag.at[POS[up + 1]], zdev(1)),
            S.copy(ag.at[POS[down]], ag.at[POS[(down + 7) % NZ]], zdev(-1)),
        ]

    def select(s):
        m = ag_t[2 * s : 2 * s + 2, :, F : F + 128].reshape(2 * G, 128).astype(F32)
        lane = lax.broadcasted_iota(jnp.int32, (1, RP), 1)
        jj = sum(jnp.where(lane >= CH * i, 1, 0) for i in range(1, NY))
        q = lane - CH * jj
        blk = jnp.where(q >= SG, 1, 0)
        slot = q - SG * blk
        yy = y + jj
        yy = jnp.where(yy >= NY, yy - NY, yy)
        expert = (z * NY + yy).astype(F32)
        row = lax.broadcasted_iota(jnp.int32, (2 * G, 1), 0)
        base = CAP * ((row & (G - 1)) >> 4)
        want = jnp.where(
            jnp.where(row >= G, 1, 0) == blk, slot - base, -1
        ).astype(F32)
        hot = jnp.zeros((2 * G, RP), F32)
        gate = jnp.zeros((2 * G, RP), F32)
        for k in range(8):
            hit = m[:, k : k + 1] == expert
            hot = jnp.where(hit, 1.0, hot)
            gate = jnp.where(hit, m[:, 8 + k : 9 + k], gate)
        rank = dot(low[...], hot.astype(BF), 1, 0)
        hot = jnp.where(rank == want, hot, 0.0)
        sel[s] = hot.astype(BF)
        gsel[s] = (hot * gate).astype(BF)

    def dispatch(s, matrix, ag, stage, rows):
        block = ag[2 * s : 2 * s + 2, :, 0:F].reshape(2 * G, F)
        out = dot(matrix[s], block, 0, 0).astype(BF).reshape(NY, CH, F)
        cps = []
        for j in range(1, NY):
            stage[s * 3 + j - 1] = out[j]
            cps.append(S.copy(stage.at[s * 3 + j - 1], rows.at[s * NY + j], ydev(j)))
        rows[s * NY] = out[0]
        return cps

    y_in = {}
    core_in, rs_in, ag_in, full_in = {}, {}, {}, {}

    def product(kind, pair):
        if kind == 0:
            a = rows_t[pl.ds(pair * NY, NY)].reshape(RP, F)
            return dot(a, wu[...], 1, 0)
        a = rows_g[pl.ds(pair * NY, NY)].reshape(RP, F)
        return dot(a, wd[...], 1, 1)

    def e1(ss, kind):
        for s in (2 * ss, 2 * ss + 1):
            for cp in y_in[s, kind]:
                cp.wait_recv()
        i = 2 * ss + kind
        cs[i] = product(kind, 2 * ss + 1 - c).astype(BF)
        core_in[ss, kind] = S.copy(cs.at[i], cr.at[i], core)
        own[kind] = product(kind, 2 * ss + c)

    def e2(ss, kind):
        i = 2 * ss + kind
        core_in[ss, kind].wait_recv()
        total = own[kind] + cr[i].astype(F32)
        rs_s[pl.ds(i * NX, NX)] = total.astype(BF).reshape(NX, CH, FF)
        rs_in[ss, kind] = [
            S.copy(rs_s.at[i * NX + (x + o) % NX], rs_r.at[i * 3 + o - 1], xdev(o))
            for o in range(1, NX)
        ]

    def spread(ss, kind, ref):
        at = (2 * ss + c) * NY + x
        ag_in[ss, kind] = [S.copy(ref.at[at], ref.at[at], xdev(o)) for o in range(1, NX)]

    def e3(ss, kind):
        i = 2 * ss + kind
        for cp in rs_in[ss, kind]:
            cp.wait_recv()
        share = rs_s[i * NX + x].astype(F32)
        for o in range(3):
            share = share + rs_r[i * 3 + o].astype(F32)
        at = (2 * ss + c) * NY + x
        if kind == 0:
            pre_sh[ss] = share
            hid[at] = (share / (1.0 + jnp.exp(-share))).astype(BF)
        else:
            pre = pre_sh[ss]
            sig = 1.0 / (1.0 + jnp.exp(-pre))
            slp[at] = (share * (sig * (1.0 + pre * (1.0 - sig)))).astype(BF)
            spread(ss, 1, slp)
            gdot[ss] = jnp.broadcast_to(
                jnp.sum(hid[at].astype(F32) * share, axis=1, keepdims=True), (CH, 128)
            )

    def e4(ss, kind, ref):
        for cp in ag_in[ss, kind]:
            cp.wait_recv()
        part_of = pl.ds((2 * ss + c) * NY, NY)
        full_in[ss, kind] = S.copy(ref.at[part_of], ref.at[part_of], core)

    def e5(ss, kind):
        full_in[ss, kind].wait_recv()

    r_in = {}

    def r1(s):
        a = slp[NY * s : NY * s + NY].reshape(RP, FF)
        out = dot(a, wu[...], 1, 1).astype(BF).reshape(NY, CH, F)
        lane = lax.broadcasted_iota(jnp.int32, (CH, 128), 1)
        r_in[s] = []
        for j in [1, 2, 3, 0]:
            here = jnp.where((c == s % 2) & (x == j), 1.0, 0.0)
            gates = jnp.where(lane == e, gdot[s // 2] * here, 0.0).astype(BF)
            if j == 0:
                ret[s * NY, :, 0:F] = out[0]
                ret[s * NY, :, F : F + 128] = gates
            else:
                st_r[s * 3 + j - 1, :, 0:F] = out[j]
                st_r[s * 3 + j - 1, :, F : F + 128] = gates
                r_in[s].append(S.copy(st_r.at[s * 3 + j - 1], ret.at[s * NY + j], ydev(-j)))

    def r2(s):
        for cp in r_in[s]:
            cp.wait_recv()
        out = dot(sel[s], ret[NY * s : NY * s + NY].reshape(RP, TM), 1, 0)
        part[2 * s : 2 * s + 2] = out.reshape(2, G, TM)

    z_in = {}

    def zsend(k, to, o, value):
        zs[k] = value.astype(BF)
        z_in[to] = S.copy(zs.at[k], zr.at[to], zdev(o))

    for cp in loc:
        cp.wait()
    for cp in in_t:
        cp.wait_recv()
    hop_t = forward(ag_t, 0)
    for cp in in_g:
        cp.wait_recv()
    hop_g = forward(ag_g, 0)
    load_u.wait()
    load_d.wait()
    for h in range(1, 5):
        s = h - 1
        for cp in hop_t:
            cp.wait_recv()
        if h < 4:
            hop_t = forward(ag_t, h)
        select(s)
        y_in[s, 0] = dispatch(s, sel, ag_t, st_t, rows_t)
        for cp in hop_g:
            cp.wait_recv()
        if h < 4:
            hop_g = forward(ag_g, h)
        y_in[s, 1] = dispatch(s, gsel, ag_g, st_g, rows_g)
        if h == 3:
            e1(0, 0)
        if h == 4:
            e2(0, 0)
            e1(0, 1)
    e2(0, 1)
    e3(0, 0)
    e1(1, 0)
    e3(0, 1)
    e2(1, 0)
    e4(0, 1, slp)
    e1(1, 1)
    e3(1, 0)
    e2(1, 1)
    e5(0, 1)
    r1(1)
    r1(0)
    e3(1, 1)
    e4(1, 1, slp)
    spread(0, 0, hid)
    spread(1, 0, hid)
    e5(1, 1)
    r1(3)
    r1(2)
    e4(0, 0, hid)
    e4(1, 0, hid)

    outs = []

    def weight_grads(lhs, rhs, width, target, base):
        for i in range(0, lhs.shape[2], width):
            n = len(outs)
            a = lhs[:, :, i : i + width].reshape(4 * RP, width)
            b = rhs[...].reshape(4 * RP, rhs.shape[2])
            cols = rhs.shape[2]
            if n >= 2:
                outs[n - 2].wait()
            gst[n % 2, 0:width, 0:cols] = dot(a, b, 0, 0).astype(BF)
            cp = pltpu.make_async_copy(
                gst.at[n % 2, pl.ds(0, width), pl.ds(0, cols)],
                target.at[pl.ds(i, width)],
                sems_l.at[base + n % 2],
            )
            cp.start()
            outs.append(cp)

    r2(1)
    r2(0)
    weight_grads(rows_t, slp, 128, gu_h, 5)
    r2(3)
    zs[4] = part[POS[4]].astype(BF)
    lo, hi = pl.ds(0, HALF), pl.ds(HALF, TM - HALF)
    z_in[3] = S.copy(zs.at[4, :, lo], zr.at[3, :, lo], zdev(-1))
    z_in[5] = S.copy(zs.at[4, :, hi], zr.at[5, :, hi], zdev(1))
    r2(2)
    z_in[3].wait_recv()
    p3 = part[POS[3]]
    zs[3, :, 0:HALF] = (p3[:, 0:HALF] + zr[3, :, 0:HALF].astype(F32)).astype(BF)
    zs[3, :, HALF:TM] = p3[:, HALF:TM].astype(BF)
    z_in[2] = S.copy(zs.at[3], zr.at[2], zdev(-1))
    z_in[5].wait_recv()
    p5 = part[POS[5]]
    zs[5, :, 0:HALF] = p5[:, 0:HALF].astype(BF)
    zs[5, :, HALF:TM] = (p5[:, HALF:TM] + zr[5, :, HALF:TM].astype(F32)).astype(BF)
    z_in[6] = S.copy(zs.at[5], zr.at[6], zdev(1))
    e5(0, 0)
    e5(1, 0)
    weight_grads(hid, rows_g, 256, gd_h, 5)
    for down, up in ((2, 6), (1, 7)):
        z_in[down].wait_recv()
        zsend(down, down - 1, -1, part[POS[down]] + zr[down].astype(F32))
        z_in[up].wait_recv()
        zsend(up, up + 1, 1, part[POS[up]] + zr[up].astype(F32))
    z_in[0].wait_recv()
    z_in[8].wait_recv()
    fin[...] = (part[POS[0]] + zr[0].astype(F32) + zr[8].astype(F32)).astype(BF).reshape(n_dp, T, TM)

    last = [S.copy(fin.at[(d + o) % n_dp], fr.at[d], dpdev(o)) for o in range(1, n_dp)]
    keep = pltpu.make_async_copy(fin.at[d], fr.at[d], sems_l.at[7])
    keep.start()
    keep.wait()
    for cp in last:
        cp.wait_recv()
    lanes = jnp.zeros((T, 128), F32)
    for i in range(n_dp):
        gt[:, i * F : (i + 1) * F] = fr[i, :, 0:F]
        lanes = lanes + fr[i, :, F : F + 128].astype(F32)
    m = meta[...].astype(F32)
    lane = lax.broadcasted_iota(jnp.int32, (T, 128), 1)
    lane_f = lane.astype(F32)
    res = jnp.zeros((T, 128), F32)
    for k in range(8):
        v = jnp.sum(jnp.where(m[:, k : k + 1] == lane_f, lanes, 0.0), axis=1, keepdims=True)
        res = jnp.where(lane == k, v / m[:, 8 + k : 9 + k], res)
    gg[...] = res
    for cp in outs[-2:]:
        cp.wait()
    for cp in S.started:
        cp.wait_send()


def local(tokens, grad_out, routes, gates, w_up, w_down):
    T, D = tokens.shape
    _, F, FF = w_up.shape
    n_dp = NX * NC
    G, CH = T * n_dp, 2 * CAP * n_dp
    RP = NY * CH
    TM = F + 128
    meta = jnp.concatenate(
        [routes.astype(BF), gates, jnp.zeros((T, 128 - 16), BF)], axis=1
    )
    vm = pl.BlockSpec(memory_space=pltpu.VMEM)
    hbm = pl.BlockSpec(memory_space=pl.ANY)
    V = pltpu.VMEM
    gt, gg, gu, gd = pl.pallas_call(
        kernel,
        out_shape=(
            jax.ShapeDtypeStruct((T, D), BF),
            jax.ShapeDtypeStruct((T, 128), F32),
            jax.ShapeDtypeStruct((F, FF), BF),
            jax.ShapeDtypeStruct((FF, F), BF),
        ),
        in_specs=[vm, vm, vm, hbm, hbm],
        out_specs=(vm, vm, hbm, hbm),
        scratch_shapes=[
            V((NZ, G, TM), BF),
            V((NZ, G, F), BF),
            V((2 * G, 2 * G), BF),
            V((4, 2 * G, RP), BF),
            V((4, 2 * G, RP), BF),
            V((12, CH, F), BF),
            V((12, CH, F), BF),
            V((16, CH, F), BF),
            V((16, CH, F), BF),
            V((F, FF), BF),
            V((FF, F), BF),
            V((2, RP, FF), F32),
            V((4, RP, FF), BF),
            V((4, RP, FF), BF),
            V((16, CH, FF), BF),
            V((12, CH, FF), BF),
            V((2, CH, FF), F32),
            V((2, CH, 128), F32),
            V((16, CH, FF), BF),
            V((16, CH, FF), BF),
            V((12, CH, TM), BF),
            V((16, CH, TM), BF),
            V((NZ, G, TM), F32),
            V((NZ, G, TM), BF),
            V((NZ + 1, G, TM), BF),
            V((n_dp, T, TM), BF),
            V((n_dp, T, TM), BF),
            V((2, 256, FF), BF),
            pltpu.SemaphoreType.DMA((140,)),
            pltpu.SemaphoreType.DMA((140,)),
            pltpu.SemaphoreType.DMA((8,)),
        ],
        compiler_params=pltpu.CompilerParams(
            collective_id=0, has_side_effects=True, vmem_limit_bytes=63 * 1024 * 1024
        ),
    )(tokens, grad_out, meta, w_up[0], w_down[0])
    return gt, gg[:, : routes.shape[1]], gu[None], gd[None]


def solution(mesh):
    rows = P(("expert", "dp"), None)
    return jax.shard_map(
        local,
        mesh=mesh,
        in_specs=(rows, rows, rows, rows, P("expert", "dp", None), P("expert", None, "dp")),
        out_specs=(rows, rows, P("expert", "dp", None), P("expert", None, "dp")),
        check_vma=False,
    )
```

```python
import functools

import jax
import jax.numpy as jnp
from jax import lax
from jax.experimental import pallas as pl
from jax.experimental.pallas import tpu as pltpu
from jax.sharding import PartitionSpec as P

MESH = pl.DeviceIdType.MESH
BF = jnp.bfloat16
F32 = jnp.float32

NZ, NY, NX, NC = 8, 4, 4, 2
CAP = 5
QUADS = ((0, 1, 7, 2), (6, 3, 5, 4))
POS = {k: 4 * q + i for q, quad in enumerate(QUADS) for i, k in enumerate(quad)}
CUT = 512


def mark(n):
    pass


def dot(a, b, ca, cb):
    return lax.dot_general(a, b, (((ca,), (cb,)), ((), ())), preferred_element_type=F32)


class Sems:
    def __init__(self, send, recv):
        self.send, self.recv, self.used, self.started = send, recv, 0, []

    def copy(self, src, dst, device):
        i = self.used
        self.used += 1
        cp = pltpu.make_async_remote_copy(
            src, dst, self.send.at[i], self.recv.at[i], device_id=device, device_id_type=MESH
        )
        cp.start()
        self.started.append(cp)
        return cp


def kernel(
    tok_h, go_h, routes, gates, wu_h, wd_h,
    gt_h, gg, gu_h, gd_h,
    tok, go, meta, ag_t, ag_g, low, sel, gsel, st_t, st_g, rows_t, rows_g, wu, wd,
    own, cs, cr, rs_s, rs_r, pre_sh, gdot, hid, slp,
    st_r, ret, part, zs, zr, fin, fr, gst,
    sems_s, sems_r, sems_l,
):
    e, d = lax.axis_index("expert"), lax.axis_index("dp")
    z, y, x, c = e // NY, e % NY, d // NC, d % NC
    n_dp = NX * NC
    T, D = tok.shape
    _, F, FH = wu.shape
    B = T * n_dp // 2
    SB = CAP * n_dp // 2
    CH = 4 * SB
    RP = NY * CH
    TM = ag_t.shape[2]

    def zdev(o):
        return (((z + o + NZ) % NZ) * NY + y, d)

    def ydev(o):
        return (z * NY + (y + o + NY) % NY, d)

    def xdev(o):
        return (e, ((x + o) % NX) * NC + c)

    core = (e, x * NC + (1 - c))

    def dpdev(o):
        return (e, (d + o) % n_dp)

    bar = pltpu.get_barrier_semaphore()
    peers = [dpdev(o) for o in range(1, n_dp)] + [zdev(1), zdev(-1)] + [ydev(o) for o in range(1, NY)]
    takes = [
        pltpu.make_async_copy(tok_h, tok, sems_l.at[10]),
        pltpu.make_async_copy(go_h, go, sems_l.at[11]),
    ]
    for cp in takes:
        cp.start()
    for p in peers:
        pl.semaphore_signal(bar, inc=1, device_id=p, device_id_type=MESH)
    loads = [
        pltpu.make_async_copy(wu_h.at[:, pl.ds(h * FH, FH)], wu.at[h], sems_l.at[h]) for h in range(2)
    ] + [
        pltpu.make_async_copy(wd_h.at[pl.ds(h * FH, FH)], wd.at[h], sems_l.at[2 + h]) for h in range(2)
    ]
    for cp in loads:
        cp.start()
    k_in = lax.broadcasted_iota(jnp.int32, (8, 128), 0)
    k_out = lax.broadcasted_iota(jnp.int32, (8, 128), 1)
    meta[...] = (
        dot(routes[...].astype(F32).astype(BF), jnp.where(k_in == k_out, 1.0, 0.0).astype(BF), 0, 0)
        + dot(gates[...], jnp.where(k_in + 8 == k_out, 1.0, 0.0).astype(BF), 0, 0)
    ).astype(BF)
    for cp in takes:
        cp.wait()
    pl.semaphore_wait(bar, len(peers))
    S = Sems(sems_s, sems_r)
    mark("bar")

    my_half = (d // NY) * NZ
    my_rows = pl.ds(pl.multiple_of((d % NY) * T, T), T)
    in_t, in_g = [], []
    for o in range(1, n_dp):
        cols = pl.ds(pl.multiple_of(((d + o) % n_dp) * F, 128), F)
        in_t.append(S.copy(meta, ag_t.at[my_half, my_rows, pl.ds(F, 128)], dpdev(o)))
        in_t.append(S.copy(tok.at[:, cols], ag_t.at[my_half, my_rows, pl.ds(0, F)], dpdev(o)))
    for o in range(1, n_dp):
        cols = pl.ds(pl.multiple_of(((d + o) % n_dp) * F, 128), F)
        in_g.append(S.copy(go.at[:, cols], ag_g.at[my_half, my_rows], dpdev(o)))
    mine = pl.ds(pl.multiple_of(d * F, 128), F)
    loc = [
        pltpu.make_async_copy(meta, ag_t.at[my_half, my_rows, pl.ds(F, 128)], sems_l.at[4]),
        pltpu.make_async_copy(tok.at[:, mine], ag_t.at[my_half, my_rows, pl.ds(0, F)], sems_l.at[5]),
        pltpu.make_async_copy(go.at[:, mine], ag_g.at[my_half, my_rows], sems_l.at[6]),
    ]
    for cp in loc:
        cp.start()
    ri = lax.broadcasted_iota(jnp.int32, (4 * B, 4 * B), 0)
    ci = lax.broadcasted_iota(jnp.int32, (4 * B, 4 * B), 1)
    same = (ri >> 4) == (ci >> 4)
    low[...] = jnp.where(same & (ci < ri), 1.0, 0.0).astype(BF)

    hops = {}

    def forward(ag, kind, a, h):
        up, down, at = h, (NZ - h) % NZ, a * NZ
        width = ag.shape[2]
        if h == 3:
            lo, hi = pl.ds(0, CUT), pl.ds(CUT, width - CUT)
            hops[kind, a] = [
                S.copy(ag.at[at + POS[up], :, lo], ag.at[at + POS[4], :, lo], zdev(1)),
                S.copy(ag.at[at + POS[down], :, hi], ag.at[at + POS[4], :, hi], zdev(-1)),
            ]
        else:
            hops[kind, a] = [
                S.copy(ag.at[at + POS[up]], ag.at[at + POS[up + 1]], zdev(1)),
                S.copy(ag.at[at + POS[down]], ag.at[at + POS[(down + 7) % NZ]], zdev(-1)),
            ]

    def hop(a, h, kind):
        for cp in hops[kind, a]:
            cp.wait_recv()
        if h < 4:
            forward((ag_t, ag_g)[kind], kind, a, h)

    def select(u):
        m = ag_t[4 * u : 4 * u + 4, :, F : F + 128].reshape(4 * B, 128).astype(F32)
        lane = lax.broadcasted_iota(jnp.int32, (1, RP), 1)
        jj = sum(jnp.where(lane >= CH * i, 1, 0) for i in range(1, NY))
        q = lane - CH * jj
        blk = sum(jnp.where(q >= SB * i, 1, 0) for i in range(1, 4))
        slot = q - SB * blk
        yy = y + jj
        yy = jnp.where(yy >= NY, yy - NY, yy)
        expert = (z * NY + yy).astype(F32)
        row = lax.broadcasted_iota(jnp.int32, (4 * B, 1), 0)
        base = CAP * ((row & (B - 1)) >> 4)
        row_blk = sum(jnp.where(row >= B * i, 1, 0) for i in range(1, 4))
        want = jnp.where(row_blk == blk, slot - base, -1).astype(F32)
        hot = jnp.zeros((4 * B, RP), F32)
        gate = jnp.zeros((4 * B, RP), F32)
        for k in range(8):
            hit = m[:, k : k + 1] == expert
            hot = jnp.where(hit, 1.0, hot)
            gate = jnp.where(hit, m[:, 8 + k : 9 + k], gate)
        rank = dot(low[...], hot.astype(BF), 1, 0)
        hot = jnp.where(rank == want, hot, 0.0)
        sel[u] = hot.astype(BF)
        gsel[u] = (hot * gate).astype(BF)

    y_in = {}
    core_in, rs_in, ag_in, full_in = {}, {}, {}, {}

    def dispatch(u, kind):
        if kind == 0:
            select(u)
        matrix, ag, stage, rows = ((sel, ag_t, st_t, rows_t), (gsel, ag_g, st_g, rows_g))[kind]
        block = ag[4 * u : 4 * u + 4, :, 0:F].reshape(4 * B, F)
        out = dot(matrix[u], block, 0, 0).astype(BF).reshape(NY, CH, F)
        y_in[u, kind] = []
        for j in range(1, NY):
            stage[u * 3 + j - 1] = out[j]
            y_in[u, kind].append(S.copy(stage.at[u * 3 + j - 1], rows.at[u * NY + j], ydev(j)))
        rows[u * NY] = out[0]

    def e1(u, kind):
        for cp in y_in[u, kind]:
            cp.wait_recv()
        i = 2 * u + kind
        a = (rows_t, rows_g)[kind][u * NY : u * NY + NY].reshape(RP, F)
        w, dim = ((wu, 0), (wd, 1))[kind]
        cs[i] = dot(a, w[1 - c], 1, dim).astype(BF)
        core_in[u, kind] = S.copy(cs.at[i], cr.at[i], core)
        own[i % 4] = dot(a, w[c], 1, dim)

    def e2(u, kind):
        i = 2 * u + kind
        core_in[u, kind].wait_recv()
        total = own[i % 4] + cr[i].astype(F32)
        rs_s[i * NX : i * NX + NX] = total.astype(BF).reshape(NX, CH, FH)
        rs_in[u, kind] = [
            S.copy(rs_s.at[i * NX + (x + o) % NX], rs_r.at[i * 3 + o - 1], xdev(o))
            for o in range(1, NX)
        ]

    def spread(u, kind):
        ref = (hid, slp)[kind]
        at = u * NY + x
        ag_in[u, kind] = [S.copy(ref.at[c, at], ref.at[c, at], xdev(o)) for o in range(1, NX)]

    def e3(u, kind):
        i = 2 * u + kind
        for cp in rs_in[u, kind]:
            cp.wait_recv()
        share = rs_s[i * NX + x].astype(F32)
        for o in range(3):
            share = share + rs_r[i * 3 + o].astype(F32)
        at = u * NY + x
        if kind == 0:
            pre_sh[u] = share
            hid[c, at] = (share / (1.0 + jnp.exp(-share))).astype(BF)
        else:
            pre = pre_sh[u]
            sig = 1.0 / (1.0 + jnp.exp(-pre))
            slp[c, at] = (share * (sig * (1.0 + pre * (1.0 - sig)))).astype(BF)
            spread(u, 1)
            gdot[u] = jnp.broadcast_to(
                jnp.sum(hid[c, at].astype(F32) * share, axis=1, keepdims=True), (CH, 128)
            )

    def e4(u, kind):
        ref = (hid, slp)[kind]
        for cp in ag_in[u, kind]:
            cp.wait_recv()
        part_of = pl.ds(u * NY, NY)
        full_in[u, kind] = S.copy(ref.at[c, part_of], ref.at[c, part_of], core)

    def e5(u, kind):
        full_in[u, kind].wait_recv()

    r_in = {}

    def r1(u):
        rows = slice(NY * u, NY * u + NY)
        out = dot(slp[0, rows].reshape(RP, FH), wu[0], 1, 1)
        out = out + dot(slp[1, rows].reshape(RP, FH), wu[1], 1, 1)
        out = out.astype(BF).reshape(NY, CH, F)
        lane = lax.broadcasted_iota(jnp.int32, (CH, 128), 1)
        r_in[u] = []
        for j in [1, 2, 3, 0]:
            here = jnp.where(x == j, 1.0, 0.0)
            dots = jnp.where(lane == e, gdot[u] * here, 0.0).astype(BF)
            if j == 0:
                ret[u * NY, :, 0:F] = out[0]
                ret[u * NY, :, F : F + 128] = dots
            else:
                st_r[u * 3 + j - 1, :, 0:F] = out[j]
                st_r[u * 3 + j - 1, :, F : F + 128] = dots
                r_in[u].append(S.copy(st_r.at[u * 3 + j - 1], ret.at[u * NY + j], ydev(-j)))

    def r2(u):
        for cp in r_in[u]:
            cp.wait_recv()
        out = dot(sel[u], ret[NY * u : NY * u + NY].reshape(RP, TM), 1, 0)
        part[4 * u : 4 * u + 4] = out.reshape(4, B, TM)

    z_in = {}

    def chain(a, step):
        p, s_at, r_at = a * NZ, a * NZ, a * (NZ + 1)
        lo, hi = pl.ds(0, CUT), pl.ds(CUT, TM - CUT)
        if step == 1:
            zs[s_at + 4] = part[p + POS[4]].astype(BF)
            z_in[a, 3] = S.copy(zs.at[s_at + 4, :, lo], zr.at[r_at + 3, :, lo], zdev(-1))
            z_in[a, 5] = S.copy(zs.at[s_at + 4, :, hi], zr.at[r_at + 5, :, hi], zdev(1))
            return
        if step == 5:
            z_in[a, 0].wait_recv()
            z_in[a, 8].wait_recv()
            total = part[p + POS[0]] + zr[r_at].astype(F32) + zr[r_at + 8].astype(F32)
            fin[a * NY : a * NY + NY] = total.astype(BF).reshape(NY, T, TM)
            return
        down, up = 5 - step, 3 + step
        z_in[a, down].wait_recv()
        if step == 2:
            mid = part[p + POS[3]]
            zs[s_at + 3, :, 0:CUT] = (mid[:, 0:CUT] + zr[r_at + 3, :, 0:CUT].astype(F32)).astype(BF)
            zs[s_at + 3, :, CUT:TM] = mid[:, CUT:TM].astype(BF)
        else:
            zs[s_at + down] = (part[p + POS[down]] + zr[r_at + down].astype(F32)).astype(BF)
        z_in[a, down - 1] = S.copy(zs.at[s_at + down], zr.at[r_at + down - 1], zdev(-1))
        z_in[a, up].wait_recv()
        if step == 2:
            mid = part[p + POS[5]]
            zs[s_at + 5, :, 0:CUT] = mid[:, 0:CUT].astype(BF)
            zs[s_at + 5, :, CUT:TM] = (mid[:, CUT:TM] + zr[r_at + 5, :, CUT:TM].astype(F32)).astype(BF)
        else:
            zs[s_at + up] = (part[p + POS[up]] + zr[r_at + up].astype(F32)).astype(BF)
        z_in[a, up + 1] = S.copy(zs.at[s_at + up], zr.at[r_at + up + 1], zdev(1))

    outs = []

    def weight_rows(kind, h, i, width):
        n = len(outs)
        if n >= 2:
            outs[n - 2].wait()
        lhs = (rows_t[:, :, i : i + width] if kind == 0 else hid[h, :, :, i : i + width])
        lhs = lhs.reshape(4 * RP, width)
        if kind == 0:
            for g in range(2):
                gst[n % 2, 0:width, g * FH : g * FH + FH] = dot(
                    lhs, slp[g].reshape(4 * RP, FH), 0, 0
                ).astype(BF)
            cp = pltpu.make_async_copy(
                gst.at[n % 2, pl.ds(0, width)], gu_h.at[pl.ds(i, width)], sems_l.at[8 + n % 2]
            )
        else:
            gst[n % 2, 0:width, 0:F] = dot(lhs, rows_g[...].reshape(4 * RP, F), 0, 0).astype(BF)
            cp = pltpu.make_async_copy(
                gst.at[n % 2, pl.ds(0, width), pl.ds(0, F)],
                gd_h.at[pl.ds(h * FH + i, width)],
                sems_l.at[8 + n % 2],
            )
        cp.start()
        outs.append(cp)

    for cp in loc:
        cp.wait()
    for cp in in_t:
        cp.wait_recv()
    forward(ag_t, 0, 0, 0)
    for cp in in_g:
        cp.wait_recv()
    forward(ag_g, 1, 0, 0)
    mark("z0")
    hop(0, 1, 0)
    hop(0, 1, 1)
    hop(0, 2, 0)
    dispatch(0, 0)
    hop(0, 2, 1)
    forward(ag_t, 0, 1, 0)
    dispatch(0, 1)
    forward(ag_g, 1, 1, 0)
    mark("d0")
    hop(0, 3, 0)
    hop(0, 3, 1)
    for cp in loads:
        cp.wait()
    hop(0, 4, 0)
    dispatch(1, 0)
    hop(0, 4, 1)
    dispatch(1, 1)
    mark("d1")
    e1(0, 0)
    hop(1, 1, 0)
    hop(1, 1, 1)
    e2(0, 0)
    e1(0, 1)
    hop(1, 2, 0)
    dispatch(2, 0)
    hop(1, 2, 1)
    dispatch(2, 1)
    mark("d2")
    e2(0, 1)
    e3(0, 0)
    spread(0, 0)
    e1(1, 0)
    hop(1, 3, 0)
    hop(1, 3, 1)
    e2(1, 0)
    e3(0, 1)
    hop(1, 4, 0)
    dispatch(3, 0)
    hop(1, 4, 1)
    dispatch(3, 1)
    mark("d3")
    e1(1, 1)
    e3(1, 0)
    e2(1, 1)
    e4(0, 1)
    e1(2, 0)
    e5(0, 1)
    e2(2, 0)
    e3(1, 1)
    mark("e3_11")
    e1(2, 1)
    e3(2, 0)
    e4(1, 1)
    e2(2, 1)
    e5(1, 1)
    e1(3, 0)
    e3(2, 1)
    e2(3, 0)
    mark("e2_30")
    r1(1)
    r1(0)
    mark("r1_0")
    e1(3, 1)
    e4(2, 1)
    e3(3, 0)
    e2(3, 1)
    mark("e2_31")
    e5(2, 1)
    e3(3, 1)
    r2(1)
    chain(0, 1)
    e4(3, 1)
    spread(1, 0)
    spread(2, 0)
    spread(3, 0)
    mark("e4_31")
    chain(0, 2)
    e5(3, 1)
    r1(3)
    r1(2)
    mark("r1_2")
    r2(0)
    chain(0, 3)
    weight_rows(0, 0, 0, 256)
    chain(0, 4)
    weight_rows(0, 0, 256, 256)
    e4(0, 0)
    chain(0, 5)
    mark("chain0")
    r2(3)
    chain(1, 1)
    for u in (1, 2, 3):
        e4(u, 0)
    mark("r2_3")
    weight_rows(0, 0, 512, 256)
    weight_rows(0, 0, 768, 128)
    chain(1, 2)
    mark("c2")
    for u in range(4):
        e5(u, 0)
    weight_rows(1, 0, 0, 256)
    r2(2)
    chain(1, 3)
    weight_rows(1, 0, 256, 256)
    weight_rows(1, 1, 0, 256)
    chain(1, 4)
    weight_rows(1, 1, 256, 256)
    mark("c4")
    chain(1, 5)
    mark("c5")

    last = [S.copy(fin.at[(d + o) % n_dp], fr.at[d], dpdev(o)) for o in range(1, n_dp)]
    keep = pltpu.make_async_copy(fin.at[d], fr.at[d], sems_l.at[7])
    keep.start()
    m = meta[...].astype(F32)
    lane = lax.broadcasted_iota(jnp.int32, (T, 128), 1).astype(F32)
    keep.wait()
    for cp in last:
        cp.wait_recv()
    stores = [
        pltpu.make_async_copy(
            fr.at[i, :, pl.ds(0, F)], gt_h.at[:, pl.ds(i * F, F)], sems_l.at[12 + i]
        )
        for i in range(n_dp)
    ]
    for cp in stores:
        cp.start()
    lanes = jnp.zeros((T, 128), F32)
    for i in range(n_dp):
        lanes = lanes + fr[i, :, F : F + 128].astype(F32)
    res = jnp.zeros((T, 128), F32)
    for k in range(8):
        v = jnp.sum(jnp.where(m[:, k : k + 1] == lane, lanes, 0.0), axis=1, keepdims=True)
        res = jnp.where(lane == k, v / m[:, 8 + k : 9 + k], res)
    gg[...] = lax.transpose(res, (1, 0))[0:8]
    for cp in outs[-2:] + stores:
        cp.wait()
    for cp in S.started:
        cp.wait_send()


def finish(*refs):
    n = (len(refs) - 2) // 3
    stage, (sin, sout) = refs[2 * n : 3 * n], refs[3 * n :]
    cps = []
    for src, mid, dst in zip(refs[:n], stage, refs[n : 2 * n]):
        rows = src.shape[0]
        step = rows // 4 if rows > 16 else rows
        for i in range(0, rows, step):
            at, k = pl.ds(i, step), len(cps)
            take = pltpu.make_async_copy(src.at[at], mid.at[at], sin.at[k])
            take.start()
            cps.append((take, pltpu.make_async_copy(mid.at[at], dst.at[at], sout.at[k])))
    for take, put in cps:
        take.wait()
        put.start()
    for take, put in cps:
        put.wait()


def local(tokens, grad_out, routes, gates, w_up, w_down):
    T, D = tokens.shape
    _, F, FF = w_up.shape
    n_dp, FH = NX * NC, FF // 2
    B, CH = T * n_dp // 2, 2 * CAP * n_dp
    RP = NY * CH
    TM = F + 128
    vm = pl.BlockSpec(memory_space=pltpu.VMEM)
    hbm = pl.BlockSpec(memory_space=pl.ANY)
    V = pltpu.VMEM
    gt, gg, gu, gd = pl.pallas_call(
        kernel,
        out_shape=(
            jax.ShapeDtypeStruct((T, D), BF),
            jax.ShapeDtypeStruct((routes.shape[1], T), F32),
            jax.ShapeDtypeStruct((F, FF), BF),
            jax.ShapeDtypeStruct((FF, F), BF),
        ),
        in_specs=[hbm, hbm, vm, vm, hbm, hbm],
        out_specs=(hbm, vm, hbm, hbm),
        scratch_shapes=[
            V((T, D), BF),
            V((T, D), BF),
            V((T, 128), BF),
            V((2 * NZ, B, TM), BF),
            V((2 * NZ, B, F), BF),
            V((4 * B, 4 * B), BF),
            V((4, 4 * B, RP), BF),
            V((4, 4 * B, RP), BF),
            V((12, CH, F), BF),
            V((12, CH, F), BF),
            V((16, CH, F), BF),
            V((16, CH, F), BF),
            V((2, F, FH), BF),
            V((2, FH, F), BF),
            V((4, RP, FH), F32),
            V((8, RP, FH), BF),
            V((8, RP, FH), BF),
            V((32, CH, FH), BF),
            V((24, CH, FH), BF),
            V((4, CH, FH), F32),
            V((4, CH, 128), F32),
            V((2, 16, CH, FH), BF),
            V((2, 16, CH, FH), BF),
            V((12, CH, TM), BF),
            V((16, CH, TM), BF),
            V((2 * NZ, B, TM), F32),
            V((2 * NZ, B, TM), BF),
            V((2 * NZ + 2, B, TM), BF),
            V((n_dp, T, TM), BF),
            V((n_dp, T, TM), BF),
            V((2, 256, FF), BF),
            pltpu.SemaphoreType.DMA((180,)),
            pltpu.SemaphoreType.DMA((180,)),
            pltpu.SemaphoreType.DMA((20,)),
        ],
        compiler_params=pltpu.CompilerParams(
            collective_id=0, has_side_effects=True, vmem_limit_bytes=63 * 1024 * 1024
        ),
    )(tokens, grad_out, routes.T, gates.T, w_up[0], w_down[0])
    made = (gt, gg, gu, gd)
    gt, gg, gu, gd = pl.pallas_call(
        finish,
        out_shape=tuple(jax.ShapeDtypeStruct(a.shape, a.dtype) for a in made),
        in_specs=[hbm] * 4,
        out_specs=(hbm,) * 4,
        scratch_shapes=[V(a.shape, a.dtype) for a in made]
        + [pltpu.SemaphoreType.DMA((16,)), pltpu.SemaphoreType.DMA((16,))],
        compiler_params=pltpu.CompilerParams(vmem_limit_bytes=63 * 1024 * 1024),
    )(*made)
    return gt, gg.T, gu[None], gd[None]


def solution(mesh):
    rows = P(("expert", "dp"), None)
    return jax.shard_map(
        local,
        mesh=mesh,
        in_specs=(rows, rows, rows, rows, P("expert", "dp", None), P("expert", None, "dp")),
        out_specs=(rows, rows, P("expert", "dp", None), P("expert", None, "dp")),
        check_vma=False,
    )
```

```python
import functools

import jax
import jax.numpy as jnp
from jax import lax
from jax.experimental import pallas as pl
from jax.experimental.pallas import tpu as pltpu
from jax.sharding import PartitionSpec as P

MESH = pl.DeviceIdType.MESH
BF = jnp.bfloat16
F32 = jnp.float32

NZ, NY, NX, NC = 8, 4, 4, 2
CAP = 5
QUADS = ((0, 1, 7, 2), (6, 3, 5, 4))
POS = {k: 4 * q + i for q, quad in enumerate(QUADS) for i, k in enumerate(quad)}
CUT = 512


def mark(n):
    pass


def dot(a, b, ca, cb):
    return lax.dot_general(a, b, (((ca,), (cb,)), ((), ())), preferred_element_type=F32)


class Sems:
    def __init__(self, send, recv):
        self.send, self.recv, self.used, self.started = send, recv, 0, []

    def copy(self, src, dst, device):
        i = self.used
        self.used += 1
        cp = pltpu.make_async_remote_copy(
            src, dst, self.send.at[i], self.recv.at[i], device_id=device, device_id_type=MESH
        )
        cp.start()
        self.started.append(cp)
        return cp


def kernel(
    tok_h, go_h, routes, gates, wu_h, wd_h,
    gt_h, gg, gu_h, gd_h,
    tok, go, meta, ag_t, ag_g, low, sel, gsel, st_t, st_g, rows_t, rows_g, wu, wd,
    own, cs, cr, rs_s, rs_r, pre_sh, gdot, hid, slp,
    st_r, ret, part, zs, zr, fin, fr, gst,
    sems_s, sems_r, sems_l,
):
    e, d = lax.axis_index("expert"), lax.axis_index("dp")
    z, y, x, c = e // NY, e % NY, d // NC, d % NC
    n_dp = NX * NC
    T, D = tok.shape
    _, F, FH = wu.shape
    B = T * n_dp // 2
    SB = CAP * n_dp // 2
    CH = 4 * SB
    RP = NY * CH
    TM = ag_t.shape[2]

    def zdev(o):
        return (((z + o + NZ) % NZ) * NY + y, d)

    def ydev(o):
        return (z * NY + (y + o + NY) % NY, d)

    def xdev(o):
        return (e, ((x + o) % NX) * NC + c)

    core = (e, x * NC + (1 - c))

    def dpdev(o):
        return (e, (d + o) % n_dp)

    bar = pltpu.get_barrier_semaphore()
    peers = [dpdev(o) for o in range(1, n_dp)] + [zdev(1), zdev(-1)] + [ydev(o) for o in range(1, NY)]
    takes = [
        pltpu.make_async_copy(tok_h, tok, sems_l.at[10]),
        pltpu.make_async_copy(go_h, go, sems_l.at[11]),
    ]
    for cp in takes:
        cp.start()
    for p in peers:
        pl.semaphore_signal(bar, inc=1, device_id=p, device_id_type=MESH)
    loads = [
        pltpu.make_async_copy(wu_h.at[:, pl.ds(h * FH, FH)], wu.at[h], sems_l.at[h]) for h in range(2)
    ] + [
        pltpu.make_async_copy(wd_h.at[pl.ds(h * FH, FH)], wd.at[h], sems_l.at[2 + h]) for h in range(2)
    ]
    for cp in loads:
        cp.start()
    k_in = lax.broadcasted_iota(jnp.int32, (8, 128), 0)
    k_out = lax.broadcasted_iota(jnp.int32, (8, 128), 1)
    meta[...] = (
        dot(routes[...].astype(F32).astype(BF), jnp.where(k_in == k_out, 1.0, 0.0).astype(BF), 0, 0)
        + dot(gates[...], jnp.where(k_in + 8 == k_out, 1.0, 0.0).astype(BF), 0, 0)
    ).astype(BF)
    for cp in takes:
        cp.wait()
    pl.semaphore_wait(bar, len(peers))
    S = Sems(sems_s, sems_r)
    mark("bar")

    my_half = (d // NY) * NZ
    my_rows = pl.ds(pl.multiple_of((d % NY) * T, T), T)
    in_t, in_g = [], []
    for o in range(1, n_dp):
        cols = pl.ds(pl.multiple_of(((d + o) % n_dp) * F, 128), F)
        in_t.append(S.copy(meta, ag_t.at[my_half, my_rows, pl.ds(F, 128)], dpdev(o)))
        in_t.append(S.copy(tok.at[:, cols], ag_t.at[my_half, my_rows, pl.ds(0, F)], dpdev(o)))
    for o in range(1, n_dp):
        cols = pl.ds(pl.multiple_of(((d + o) % n_dp) * F, 128), F)
        in_g.append(S.copy(go.at[:, cols], ag_g.at[my_half, my_rows], dpdev(o)))
    mine = pl.ds(pl.multiple_of(d * F, 128), F)
    loc = [
        pltpu.make_async_copy(meta, ag_t.at[my_half, my_rows, pl.ds(F, 128)], sems_l.at[4]),
        pltpu.make_async_copy(tok.at[:, mine], ag_t.at[my_half, my_rows, pl.ds(0, F)], sems_l.at[5]),
        pltpu.make_async_copy(go.at[:, mine], ag_g.at[my_half, my_rows], sems_l.at[6]),
    ]
    for cp in loc:
        cp.start()
    ri = lax.broadcasted_iota(jnp.int32, (4 * B, 4 * B), 0)
    ci = lax.broadcasted_iota(jnp.int32, (4 * B, 4 * B), 1)
    same = (ri >> 4) == (ci >> 4)
    low[...] = jnp.where(same & (ci < ri), 1.0, 0.0).astype(BF)

    hops = {}

    def forward(ag, kind, a, h):
        up, down, at = h, (NZ - h) % NZ, a * NZ
        width = ag.shape[2]
        if h == 3:
            lo, hi = pl.ds(0, CUT), pl.ds(CUT, width - CUT)
            hops[kind, a] = [
                S.copy(ag.at[at + POS[up], :, lo], ag.at[at + POS[4], :, lo], zdev(1)),
                S.copy(ag.at[at + POS[down], :, hi], ag.at[at + POS[4], :, hi], zdev(-1)),
            ]
        else:
            hops[kind, a] = [
                S.copy(ag.at[at + POS[up]], ag.at[at + POS[up + 1]], zdev(1)),
                S.copy(ag.at[at + POS[down]], ag.at[at + POS[(down + 7) % NZ]], zdev(-1)),
            ]

    def hop(a, h, kind):
        for cp in hops[kind, a]:
            cp.wait_recv()
        if h < 4:
            forward((ag_t, ag_g)[kind], kind, a, h)

    def select(u):
        m = ag_t[4 * u : 4 * u + 4, :, F : F + 128].reshape(4 * B, 128).astype(F32)
        lane = lax.broadcasted_iota(jnp.int32, (1, RP), 1)
        jj = sum(jnp.where(lane >= CH * i, 1, 0) for i in range(1, NY))
        q = lane - CH * jj
        blk = sum(jnp.where(q >= SB * i, 1, 0) for i in range(1, 4))
        slot = q - SB * blk
        yy = y + jj
        yy = jnp.where(yy >= NY, yy - NY, yy)
        expert = (z * NY + yy).astype(F32)
        row = lax.broadcasted_iota(jnp.int32, (4 * B, 1), 0)
        base = CAP * ((row & (B - 1)) >> 4)
        row_blk = sum(jnp.where(row >= B * i, 1, 0) for i in range(1, 4))
        want = jnp.where(row_blk == blk, slot - base, -1).astype(F32)
        hot = jnp.zeros((4 * B, RP), F32)
        gate = jnp.zeros((4 * B, RP), F32)
        for k in range(8):
            hit = m[:, k : k + 1] == expert
            hot = jnp.where(hit, 1.0, hot)
            gate = jnp.where(hit, m[:, 8 + k : 9 + k], gate)
        rank = dot(low[...], hot.astype(BF), 1, 0)
        hot = jnp.where(rank == want, hot, 0.0)
        sel[u] = hot.astype(BF)
        gsel[u] = (hot * gate).astype(BF)

    y_in = {}
    core_in, rs_in, ag_in, full_in = {}, {}, {}, {}

    def dispatch(u, kind):
        if kind == 0:
            select(u)
        matrix, ag, stage, rows = ((sel, ag_t, st_t, rows_t), (gsel, ag_g, st_g, rows_g))[kind]
        block = ag[4 * u : 4 * u + 4, :, 0:F].reshape(4 * B, F)
        out = dot(matrix[u], block, 0, 0).astype(BF).reshape(NY, CH, F)
        y_in[u, kind] = []
        for j in range(1, NY):
            stage[u * 3 + j - 1] = out[j]
            y_in[u, kind].append(S.copy(stage.at[u * 3 + j - 1], rows.at[u * NY + j], ydev(j)))
        rows[u * NY] = out[0]

    def e1(u, kind):
        for cp in y_in[u, kind]:
            cp.wait_recv()
        i = 2 * u + kind
        a = (rows_t, rows_g)[kind][u * NY : u * NY + NY].reshape(RP, F)
        w, dim = ((wu, 0), (wd, 1))[kind]
        cs[i] = dot(a, w[1 - c], 1, dim).astype(BF)
        core_in[u, kind] = S.copy(cs.at[i], cr.at[i], core)
        own[i % 4] = dot(a, w[c], 1, dim)

    def e2(u, kind):
        i = 2 * u + kind
        core_in[u, kind].wait_recv()
        total = own[i % 4] + cr[i].astype(F32)
        rs_s[i * NX : i * NX + NX] = total.astype(BF).reshape(NX, CH, FH)
        rs_in[u, kind] = [
            S.copy(rs_s.at[i * NX + (x + o) % NX], rs_r.at[i * 3 + o - 1], xdev(o))
            for o in range(1, NX)
        ]

    def spread(u, kind):
        ref = (hid, slp)[kind]
        at = u * NY + x
        ag_in[u, kind] = [S.copy(ref.at[c, at], ref.at[c, at], xdev(o)) for o in range(1, NX)]

    def e3(u, kind):
        i = 2 * u + kind
        for cp in rs_in[u, kind]:
            cp.wait_recv()
        share = rs_s[i * NX + x].astype(F32)
        for o in range(3):
            share = share + rs_r[i * 3 + o].astype(F32)
        at = u * NY + x
        if kind == 0:
            pre_sh[u] = share
            hid[c, at] = (share / (1.0 + jnp.exp(-share))).astype(BF)
        else:
            pre = pre_sh[u]
            sig = 1.0 / (1.0 + jnp.exp(-pre))
            slp[c, at] = (share * (sig * (1.0 + pre * (1.0 - sig)))).astype(BF)
            spread(u, 1)
            gdot[u] = jnp.broadcast_to(
                jnp.sum(hid[c, at].astype(F32) * share, axis=1, keepdims=True), (CH, 128)
            )

    def e4(u, kind):
        ref = (hid, slp)[kind]
        for cp in ag_in[u, kind]:
            cp.wait_recv()
        part_of = pl.ds(u * NY, NY)
        full_in[u, kind] = S.copy(ref.at[c, part_of], ref.at[c, part_of], core)

    def e5(u, kind):
        full_in[u, kind].wait_recv()

    r_in = {}

    def r1(u):
        rows = slice(NY * u, NY * u + NY)
        out = dot(slp[0, rows].reshape(RP, FH), wu[0], 1, 1)
        out = out + dot(slp[1, rows].reshape(RP, FH), wu[1], 1, 1)
        out = out.astype(BF).reshape(NY, CH, F)
        lane = lax.broadcasted_iota(jnp.int32, (CH, 128), 1)
        r_in[u] = []
        for j in [1, 2, 3, 0]:
            here = jnp.where(x == j, 1.0, 0.0)
            dots = jnp.where(lane == e, gdot[u] * here, 0.0).astype(BF)
            if j == 0:
                ret[u * NY, :, 0:F] = out[0]
                ret[u * NY, :, F : F + 128] = dots
            else:
                st_r[u * 3 + j - 1, :, 0:F] = out[j]
                st_r[u * 3 + j - 1, :, F : F + 128] = dots
                r_in[u].append(S.copy(st_r.at[u * 3 + j - 1], ret.at[u * NY + j], ydev(-j)))

    def r2(u):
        for cp in r_in[u]:
            cp.wait_recv()
        out = dot(sel[u], ret[NY * u : NY * u + NY].reshape(RP, TM), 1, 0)
        part[4 * u : 4 * u + 4] = out.reshape(4, B, TM)

    z_in = {}

    def chain(a, step):
        p, s_at, r_at = a * NZ, a * NZ, a * (NZ + 1)
        lo, hi = pl.ds(0, CUT), pl.ds(CUT, TM - CUT)
        if step == 1:
            zs[s_at + 4] = part[p + POS[4]].astype(BF)
            z_in[a, 3] = S.copy(zs.at[s_at + 4, :, lo], zr.at[r_at + 3, :, lo], zdev(-1))
            z_in[a, 5] = S.copy(zs.at[s_at + 4, :, hi], zr.at[r_at + 5, :, hi], zdev(1))
            return
        if step == 5:
            z_in[a, 0].wait_recv()
            z_in[a, 8].wait_recv()
            total = part[p + POS[0]] + zr[r_at].astype(F32) + zr[r_at + 8].astype(F32)
            fin[a * NY : a * NY + NY] = total.astype(BF).reshape(NY, T, TM)
            return
        down, up = 5 - step, 3 + step
        z_in[a, down].wait_recv()
        if step == 2:
            mid = part[p + POS[3]]
            zs[s_at + 3, :, 0:CUT] = (mid[:, 0:CUT] + zr[r_at + 3, :, 0:CUT].astype(F32)).astype(BF)
            zs[s_at + 3, :, CUT:TM] = mid[:, CUT:TM].astype(BF)
        else:
            zs[s_at + down] = (part[p + POS[down]] + zr[r_at + down].astype(F32)).astype(BF)
        z_in[a, down - 1] = S.copy(zs.at[s_at + down], zr.at[r_at + down - 1], zdev(-1))
        z_in[a, up].wait_recv()
        if step == 2:
            mid = part[p + POS[5]]
            zs[s_at + 5, :, 0:CUT] = mid[:, 0:CUT].astype(BF)
            zs[s_at + 5, :, CUT:TM] = (mid[:, CUT:TM] + zr[r_at + 5, :, CUT:TM].astype(F32)).astype(BF)
        else:
            zs[s_at + up] = (part[p + POS[up]] + zr[r_at + up].astype(F32)).astype(BF)
        z_in[a, up + 1] = S.copy(zs.at[s_at + up], zr.at[r_at + up + 1], zdev(1))

    outs = []

    def weight_rows(kind, h, i, width):
        n = len(outs)
        if n >= 2:
            outs[n - 2].wait()
        lhs = (rows_t[:, :, i : i + width] if kind == 0 else hid[h, :, :, i : i + width])
        lhs = lhs.reshape(4 * RP, width)
        if kind == 0:
            for g in range(2):
                gst[n % 2, 0:width, g * FH : g * FH + FH] = dot(
                    lhs, slp[g].reshape(4 * RP, FH), 0, 0
                ).astype(BF)
            cp = pltpu.make_async_copy(
                gst.at[n % 2, pl.ds(0, width)], gu_h.at[pl.ds(i, width)], sems_l.at[8 + n % 2]
            )
        else:
            gst[n % 2, 0:width, 0:F] = dot(lhs, rows_g[...].reshape(4 * RP, F), 0, 0).astype(BF)
            cp = pltpu.make_async_copy(
                gst.at[n % 2, pl.ds(0, width), pl.ds(0, F)],
                gd_h.at[pl.ds(h * FH + i, width)],
                sems_l.at[8 + n % 2],
            )
        cp.start()
        outs.append(cp)

    for cp in loc:
        cp.wait()
    for cp in in_t:
        cp.wait_recv()
    forward(ag_t, 0, 0, 0)
    for cp in in_g:
        cp.wait_recv()
    forward(ag_g, 1, 0, 0)
    mark("z0")
    hop(0, 1, 0)
    hop(0, 1, 1)
    hop(0, 2, 0)
    dispatch(0, 0)
    hop(0, 2, 1)
    dispatch(0, 1)
    mark("d0")
    hop(0, 3, 0)
    hop(0, 3, 1)
    forward(ag_t, 0, 1, 0)
    forward(ag_g, 1, 1, 0)
    for cp in loads:
        cp.wait()
    hop(0, 4, 0)
    dispatch(1, 0)
    hop(0, 4, 1)
    dispatch(1, 1)
    mark("d1")
    e1(0, 0)
    hop(1, 1, 0)
    hop(1, 1, 1)
    e2(0, 0)
    e1(0, 1)
    hop(1, 2, 0)
    dispatch(2, 0)
    hop(1, 2, 1)
    dispatch(2, 1)
    mark("d2")
    e2(0, 1)
    e3(0, 0)
    spread(0, 0)
    e1(1, 0)
    hop(1, 3, 0)
    hop(1, 3, 1)
    e2(1, 0)
    e3(0, 1)
    hop(1, 4, 0)
    dispatch(3, 0)
    hop(1, 4, 1)
    dispatch(3, 1)
    mark("d3")
    e1(1, 1)
    e3(1, 0)
    e2(1, 1)
    e4(0, 1)
    e1(2, 0)
    e5(0, 1)
    e2(2, 0)
    e3(1, 1)
    mark("e3_11")
    e1(2, 1)
    e3(2, 0)
    e4(1, 1)
    e2(2, 1)
    e5(1, 1)
    e1(3, 0)
    e3(2, 1)
    e2(3, 0)
    mark("e2_30")
    r1(1)
    r1(0)
    mark("r1_0")
    e1(3, 1)
    e4(2, 1)
    e3(3, 0)
    e2(3, 1)
    mark("e2_31")
    e5(2, 1)
    e3(3, 1)
    r2(1)
    chain(0, 1)
    e4(3, 1)
    spread(1, 0)
    spread(2, 0)
    spread(3, 0)
    mark("e4_31")
    chain(0, 2)
    e5(3, 1)
    r1(3)
    r1(2)
    mark("r1_2")
    r2(0)
    chain(0, 3)
    weight_rows(0, 0, 0, 256)
    chain(0, 4)
    weight_rows(0, 0, 256, 256)
    e4(0, 0)
    chain(0, 5)
    mark("chain0")
    r2(3)
    chain(1, 1)
    for u in (1, 2, 3):
        e4(u, 0)
    mark("r2_3")
    weight_rows(0, 0, 512, 256)
    weight_rows(0, 0, 768, 128)
    chain(1, 2)
    mark("c2")
    for u in range(4):
        e5(u, 0)
    weight_rows(1, 0, 0, 256)
    r2(2)
    chain(1, 3)
    weight_rows(1, 0, 256, 256)
    weight_rows(1, 1, 0, 256)
    chain(1, 4)
    weight_rows(1, 1, 256, 256)
    mark("c4")
    chain(1, 5)
    mark("c5")

    last = [S.copy(fin.at[(d + o) % n_dp], fr.at[d], dpdev(o)) for o in range(1, n_dp)]
    keep = pltpu.make_async_copy(fin.at[d], fr.at[d], sems_l.at[7])
    keep.start()
    m = meta[...].astype(F32)
    lane = lax.broadcasted_iota(jnp.int32, (T, 128), 1).astype(F32)
    keep.wait()
    for cp in last:
        cp.wait_recv()
    stores = [
        pltpu.make_async_copy(
            fr.at[i, :, pl.ds(0, F)], gt_h.at[:, pl.ds(i * F, F)], sems_l.at[12 + i]
        )
        for i in range(n_dp)
    ]
    for cp in stores:
        cp.start()
    lanes = jnp.zeros((T, 128), F32)
    for i in range(n_dp):
        lanes = lanes + fr[i, :, F : F + 128].astype(F32)
    res = jnp.zeros((T, 128), F32)
    for k in range(8):
        v = jnp.sum(jnp.where(m[:, k : k + 1] == lane, lanes, 0.0), axis=1, keepdims=True)
        res = jnp.where(lane == k, v / m[:, 8 + k : 9 + k], res)
    gg[...] = lax.transpose(res, (1, 0))[0:8]
    for cp in outs[-2:] + stores:
        cp.wait()
    for cp in S.started:
        cp.wait_send()


def finish(*refs):
    n = (len(refs) - 2) // 3
    stage, (sin, sout) = refs[2 * n : 3 * n], refs[3 * n :]
    cps = []
    for src, mid, dst in zip(refs[:n], stage, refs[n : 2 * n]):
        rows = src.shape[0]
        step = rows // 4 if rows > 16 else rows
        for i in range(0, rows, step):
            at, k = pl.ds(i, step), len(cps)
            take = pltpu.make_async_copy(src.at[at], mid.at[at], sin.at[k])
            take.start()
            cps.append((take, pltpu.make_async_copy(mid.at[at], dst.at[at], sout.at[k])))
    for take, put in cps:
        take.wait()
        put.start()
    for take, put in cps:
        put.wait()


def local(tokens, grad_out, routes, gates, w_up, w_down):
    T, D = tokens.shape
    _, F, FF = w_up.shape
    n_dp, FH = NX * NC, FF // 2
    B, CH = T * n_dp // 2, 2 * CAP * n_dp
    RP = NY * CH
    TM = F + 128
    vm = pl.BlockSpec(memory_space=pltpu.VMEM)
    hbm = pl.BlockSpec(memory_space=pl.ANY)
    V = pltpu.VMEM
    gt, gg, gu, gd = pl.pallas_call(
        kernel,
        out_shape=(
            jax.ShapeDtypeStruct((T, D), BF),
            jax.ShapeDtypeStruct((routes.shape[1], T), F32),
            jax.ShapeDtypeStruct((F, FF), BF),
            jax.ShapeDtypeStruct((FF, F), BF),
        ),
        in_specs=[hbm, hbm, vm, vm, hbm, hbm],
        out_specs=(hbm, vm, hbm, hbm),
        scratch_shapes=[
            V((T, D), BF),
            V((T, D), BF),
            V((T, 128), BF),
            V((2 * NZ, B, TM), BF),
            V((2 * NZ, B, F), BF),
            V((4 * B, 4 * B), BF),
            V((4, 4 * B, RP), BF),
            V((4, 4 * B, RP), BF),
            V((12, CH, F), BF),
            V((12, CH, F), BF),
            V((16, CH, F), BF),
            V((16, CH, F), BF),
            V((2, F, FH), BF),
            V((2, FH, F), BF),
            V((4, RP, FH), F32),
            V((8, RP, FH), BF),
            V((8, RP, FH), BF),
            V((32, CH, FH), BF),
            V((24, CH, FH), BF),
            V((4, CH, FH), F32),
            V((4, CH, 128), F32),
            V((2, 16, CH, FH), BF),
            V((2, 16, CH, FH), BF),
            V((12, CH, TM), BF),
            V((16, CH, TM), BF),
            V((2 * NZ, B, TM), F32),
            V((2 * NZ, B, TM), BF),
            V((2 * NZ + 2, B, TM), BF),
            V((n_dp, T, TM), BF),
            V((n_dp, T, TM), BF),
            V((2, 256, FF), BF),
            pltpu.SemaphoreType.DMA((180,)),
            pltpu.SemaphoreType.DMA((180,)),
            pltpu.SemaphoreType.DMA((20,)),
        ],
        compiler_params=pltpu.CompilerParams(
            collective_id=0, has_side_effects=True, vmem_limit_bytes=63 * 1024 * 1024
        ),
    )(tokens, grad_out, routes.T, gates.T, w_up[0], w_down[0])
    made = (gt, gg, gu, gd)
    gt, gg, gu, gd = pl.pallas_call(
        finish,
        out_shape=tuple(jax.ShapeDtypeStruct(a.shape, a.dtype) for a in made),
        in_specs=[hbm] * 4,
        out_specs=(hbm,) * 4,
        scratch_shapes=[V(a.shape, a.dtype) for a in made]
        + [pltpu.SemaphoreType.DMA((16,)), pltpu.SemaphoreType.DMA((16,))],
        compiler_params=pltpu.CompilerParams(vmem_limit_bytes=63 * 1024 * 1024),
    )(*made)
    return gt, gg.T, gu[None], gd[None]


def solution(mesh):
    rows = P(("expert", "dp"), None)
    return jax.shard_map(
        local,
        mesh=mesh,
        in_specs=(rows, rows, rows, rows, P("expert", "dp", None), P("expert", None, "dp")),
        out_specs=(rows, rows, P("expert", "dp", None), P("expert", None, "dp")),
        check_vma=False,
    )
```
